512 devices in a mesh: dp: 64 (over z, x, core), seq: 8 (over y).
Axes of the slice: x: 4, y: 8, z: 8, core: 2. Of those that a mesh axis runs over, the one named last changes fastest.
Arguments:
- queries: bfloat16 [65536, 4096], P(('dp', 'seq')), may hold values from -6 to 6
- keys: bfloat16 [65536, 512], P(('dp', 'seq')), may hold values from -6 to 6
- values: bfloat16 [65536, 512], P(('dp', 'seq')), may hold values from -6 to 6
- grad_out: bfloat16 [65536, 4096], P(('dp', 'seq')), may hold values from -6 to 6
- quant_scale: float32 [2, 4, 128], replicated, may hold values from 2 to 8
- doc_lengths: int32 [64, 8], P('dp'), may hold values from 1 to 512, as said below
Outputs:
- attn_out: bfloat16 [65536, 4096], P(('dp', 'seq'))
- grad_queries: bfloat16 [65536, 4096], P(('dp', 'seq'))
- grad_keys: bfloat16 [65536, 512], P(('dp', 'seq'))
- grad_values: bfloat16 [65536, 512], P(('dp', 'seq'))
- grad_scale: float32 [2, 4, 128], replicated
The draws below stay inside these ranges and needn't reach their ends.
Inputs may be any that keep to these rules, and one draw needn't show every extreme that they name: `doc_lengths`: each row sums to 1024; its largest length is exactly 512.
All inputs are finite; a program needn't handle non-finite values.
Results may differ from the reference program's by a relative error of at most 0.04.
Values may be sent and summed in bfloat16 or wider, within the bound.
A program may use at most 64 MiB of HBM per device.

```python
import math
import jax
import jax.numpy as jnp
from jax import lax

HQ = 32
KVH = 4
HD = 128
DOCS = 8
SLAB = 1024
ROWS = 65536
N_DP = 64


def doc_table(key):
    key = jax.random.fold_in(key, 101)
    half = SLAB // 2
    rest = SLAB - half

    def one_slab(slab_key):
        pick_key, cut_key = jax.random.split(slab_key)
        biggest = jax.random.randint(pick_key, (), 0, DOCS, dtype=jnp.int32)
        order = jax.random.permutation(cut_key, rest - 1).astype(jnp.int32) + 1
        chosen = order[:DOCS - 2]
        ascending = -lax.top_k(-chosen, DOCS - 2)[0]
        bounds = jnp.concatenate([jnp.zeros((1,), jnp.int32), ascending, jnp.full((1,), rest, jnp.int32)])
        others = bounds[1:] - bounds[:-1]
        index = jnp.arange(DOCS, dtype=jnp.int32)
        source = jnp.clip(jnp.where(index < biggest, index, index - 1), 0, DOCS - 2)
        lengths = jnp.where(index == biggest, half, others[source]).astype(jnp.int32)
        first = jnp.sum(jnp.where(index < biggest, lengths, 0)).astype(jnp.int32)
        return (lengths, first)
    return jax.vmap(one_slab)(jax.random.split(key, N_DP))


def draw_doc_lengths(key, part):
    lengths, starts = doc_table(key)
    return lengths


def draw_queries(key, part):
    key = jax.random.fold_in(key, 3)
    return jax.random.truncated_normal(key, -6.0, 6.0, (ROWS, HQ * HD), jnp.float32).astype(jnp.bfloat16)


def draw_keys(key, part):
    key = jax.random.fold_in(key, 5)
    return jax.random.truncated_normal(key, -6.0, 6.0, (ROWS, KVH * HD), jnp.float32).astype(jnp.bfloat16)


def level_of(own_key, extent, pieces, smallest, top_value):
    factor_of, own = 1.0, jax.random.fold_in(own_key, 6)
    for axis_at, blocks in pieces:
        draws = jnp.exp(jax.random.uniform(jax.random.fold_in(own, axis_at), (blocks,), jnp.float32, smallest / len(pieces), top_value / len(pieces)))
        factor_of = factor_of * jnp.repeat(draws, extent[axis_at] // blocks).reshape([-1 if axis == axis_at else 1 for axis in range(len(extent))])
    return factor_of


def normal_values(rng, shape, deviation, reach, pieces=(), held_as=jnp.bfloat16):
    drawn = deviation * jax.random.normal(rng, shape, jnp.float32)
    if pieces:
        drawn = drawn * level_of(rng, shape, pieces, -0.22, 0.18)
    return jnp.clip(drawn, -reach, reach).astype(held_as)


def setup_inputs(seed: int = 0) -> dict:
    splits = jax.random.split(jax.random.key(seed), 7)
    queries = draw_queries(jax.random.fold_in(splits[6], 71), 0)
    keys = draw_keys(jax.random.fold_in(splits[6], 71), 0)
    values = normal_values(splits[2], (ROWS, KVH * HD), 1.0, 6.0, ((0, 512),))
    grad_out = normal_values(splits[3], (ROWS, HQ * HD), 1.0, 6.0, ((0, 512),))
    quant_scale = jnp.clip(jnp.exp(jax.random.uniform(splits[4], (2, KVH, HD), jnp.float32, math.log(2.0), math.log(8.0))), 2.0, 8.0)
    doc_lengths = draw_doc_lengths(jax.random.fold_in(splits[6], 71), 0)
    return dict(queries=queries, keys=keys, values=values, grad_out=grad_out, quant_scale=quant_scale, doc_lengths=doc_lengths)


two_pi = 2.0 * math.pi

def quantize(source, clip):
    level = 127.0 * jnp.tanh(source / clip)
    return clip / 127.0 * (level - jnp.sin(two_pi * level) / two_pi)

def quant_pair(key_raw, value_raw, clip):
    return (quantize(key_raw, clip[0]), quantize(value_raw, clip[1]))

def segments(lengths, length):
    ends = jnp.cumsum(lengths.astype(jnp.int32))
    positions = jnp.arange(length, dtype=jnp.int32)
    return lax.optimization_barrier(jnp.sum((positions[:, None] >= ends[None, :]).astype(jnp.int32), axis=1))

def attend(query_rows, key_rows, value_rows, grad_rows, segment, row_start, local_kv):
    length = query_rows.shape[0]
    key_len = key_rows.shape[0]
    head_dim = key_rows.shape[1] // local_kv
    per_group = query_rows.shape[1] // (local_kv * head_dim)
    query4 = query_rows.reshape(length, local_kv, per_group, head_dim).astype(jnp.float32)
    grad4 = grad_rows.reshape(length, local_kv, per_group, head_dim)
    key3 = key_rows.reshape(key_len, local_kv, head_dim).astype(jnp.float32)
    value3 = value_rows.reshape(key_len, local_kv, head_dim).astype(jnp.float32)
    block = min(512, length)
    scale = head_dim ** (-0.5)
    columns = jnp.arange(key_len, dtype=jnp.int32)

    def step(carry, index):
        key_acc, value_acc = carry
        start = (index * block).astype(jnp.int32)
        query_blk = lax.dynamic_slice_in_dim(query4, start, block, 0)
        grad_blk = lax.dynamic_slice_in_dim(grad4, start, block, 0)
        row_ids = row_start + start + jnp.arange(block, dtype=jnp.int32)
        row_seg = lax.dynamic_slice_in_dim(segment, row_start + start, block, 0)
        allowed = (columns[None, :] <= row_ids[:, None]) & (segment[None, :] == row_seg[:, None])
        scores = jnp.einsum('qngd,knd->ngqk', query_blk, key3) * scale
        scores = jnp.where(allowed, scores, -1e+30)
        weights = jnp.exp(scores - lax.optimization_barrier(jnp.max(scores, axis=-1, keepdims=True)))
        probs = weights / lax.optimization_barrier(jnp.sum(weights, axis=-1, keepdims=True))
        probs_b = probs.astype(jnp.bfloat16)
        output = jnp.einsum('ngqk,knd->qngd', probs_b.astype(jnp.float32), value3).astype(jnp.bfloat16)
        grad_f = grad_blk.astype(jnp.float32)
        delta = jnp.transpose(lax.optimization_barrier(jnp.sum(grad_f * output.astype(jnp.float32), axis=-1)), (1, 2, 0))
        dprob = jnp.einsum('qngd,knd->ngqk', grad_f, value3)
        dscore = (probs * (dprob - delta[..., None]) * scale).astype(jnp.bfloat16)
        dscore_f = dscore.astype(jnp.float32)
        grad_query = jnp.einsum('ngqk,knd->qngd', dscore_f, key3).astype(jnp.bfloat16)
        key_acc = key_acc + jnp.einsum('ngqk,qngd->knd', dscore_f, query_blk)
        value_acc = value_acc + jnp.einsum('ngqk,qngd->knd', probs_b.astype(jnp.float32), grad_f)
        return ((key_acc, value_acc), (output, grad_query))
    zeros = jnp.zeros((key_len, local_kv, head_dim), jnp.float32)
    (key_grad, value_grad), (outputs, grad_query) = lax.scan(step, (zeros, zeros), jnp.arange(length // block, dtype=jnp.int32))
    return (outputs.reshape(length, -1), grad_query.reshape(length, -1), key_grad.reshape(key_len, -1), value_grad.reshape(key_len, -1))

def reference(queries, keys, values, grad_out, quant_scale, doc_lengths):
    rows = queries.shape[0]
    key_raw = keys.astype(jnp.float32).reshape(rows, KVH, HD)
    value_raw = values.astype(jnp.float32).reshape(rows, KVH, HD)
    (key_q, value_q), pull = jax.vjp(quant_pair, key_raw, value_raw, quant_scale)
    key_b = key_q.astype(jnp.bfloat16).reshape(N_DP, SLAB, KVH * HD)
    value_b = value_q.astype(jnp.bfloat16).reshape(N_DP, SLAB, KVH * HD)

    def per_slab(item):
        query_rows, key_rows, value_rows, grad_rows, lengths = item
        segment = segments(lengths, SLAB)
        return attend(query_rows, key_rows, value_rows, grad_rows, segment, 0, KVH)
    outputs, grad_query, key_grad, value_grad = lax.map(per_slab, (queries.reshape(N_DP, SLAB, HQ * HD), key_b, value_b, grad_out.reshape(N_DP, SLAB, HQ * HD), doc_lengths))
    key_in, value_in, grad_scale = pull((key_grad.reshape(rows, KVH, HD), value_grad.reshape(rows, KVH, HD)))
    return (outputs.reshape(rows, HQ * HD), grad_query.reshape(rows, HQ * HD), key_in.reshape(rows, KVH * HD).astype(jnp.bfloat16), value_in.reshape(rows, KVH * HD).astype(jnp.bfloat16), grad_scale)
```

```python
import functools
import math

import jax
import jax.numpy as jnp
from jax import lax
from jax.experimental import pallas as pl
from jax.experimental.pallas import tpu as pltpu
from jax.sharding import PartitionSpec as P

MESH = pl.DeviceIdType.MESH
HD = 128
BACK = 4
WIN = (BACK + 1) * HD
GROUP = 2
SCALE = HD**-0.5


def transposed_lhs(a, b):
    return lax.dot_general(a, b, (((0,), (0,)), ((), ())), preferred_element_type=jnp.float32)


def dot_nt(a, b):
    return lax.dot_general(a, b, (((1,), (1,)), ((), ())), preferred_element_type=jnp.float32)


def dot(a, b):
    return jnp.dot(a, b, preferred_element_type=jnp.float32)


def quantize(x, c):
    ratio = x / c
    t = jnp.tanh(ratio)
    u = 127.0 * t
    angle = math.pi * (u - jnp.floor(u + 0.5))
    s = jnp.sin(angle)
    level = u - s * jnp.cos(angle) * (1.0 / math.pi)
    by_x = (1.0 - t * t) * (2.0 * s * s)
    return (c * (1.0 / 127.0)) * level, by_x, level * (1.0 / 127.0) - ratio * by_x


def attend_step(q, g, keys, values, bias):
    rows = q.shape[0]
    s = dot_nt(q, keys) * (SCALE * math.log2(math.e))
    s = (s.reshape(rows // HD, HD, WIN) + bias[None]).reshape(rows, WIN)
    p = jnp.exp2(s - jnp.max(s, axis=1, keepdims=True))
    inv = 1.0 / jnp.sum(p, axis=1, keepdims=True)
    p_b = p.astype(jnp.bfloat16)
    out = dot(p_b, values) * inv
    g_n = (g.astype(jnp.float32) * inv).astype(jnp.bfloat16)
    delta = jnp.sum(g_n.astype(jnp.float32) * out, axis=1, keepdims=True)
    ds = (p * (dot_nt(g_n, values) - delta)).astype(jnp.bfloat16)
    dq = dot(ds, keys) * SCALE
    return out, dq, transposed_lhs(q, ds), transposed_lhs(g_n, p_b)


def kernel(
    kvh, q_hbm, g_hbm, k_ref, v_ref, clip_ref, doc_ref,
    o_hbm, dq_hbm, gk_ref, gv_ref, gs_ref,
    q_buf, g_buf, o_buf, dq_buf, kv, part, sbuf, rbuf, bias, dx, dc, ar_src, ar_buf,
    in_sem, out_sem, fs, fr, bs, br, ars, arr,
):
    n_seq, n_dp = lax.axis_size("seq"), lax.axis_size("dp")
    me, dp = lax.axis_index("seq"), lax.axis_index("dp")
    n_w = min(8, n_dp)
    n_z = n_dp // n_w
    w, z = lax.rem(dp, n_w), dp // n_w
    nxt, prv = lax.rem(me + 1, n_seq), lax.rem(me + n_seq - 1, n_seq)
    per_kv = q_hbm.shape[1] // kvh

    def columns(h):
        return pl.ds(pl.multiple_of(h * per_kv, HD), per_kv)

    def loads(h):
        return (
            pltpu.make_async_copy(q_hbm.at[:, columns(h)], q_buf.at[h], in_sem.at[h, 0]),
            pltpu.make_async_copy(g_hbm.at[:, columns(h)], g_buf.at[h], in_sem.at[h, 1]),
        )

    def stores(h):
        return (
            pltpu.make_async_copy(o_buf.at[h], o_hbm.at[:, columns(h)], out_sem.at[h, 0]),
            pltpu.make_async_copy(dq_buf.at[h], dq_hbm.at[:, columns(h)], out_sem.at[h, 1]),
        )

    for h in range(kvh):
        for copy in loads(h):
            copy.start()

    phases = []
    for mine, count, where in (
        (me, n_seq, lambda i: {"seq": i}),
        (w, n_w, lambda i: {"dp": z * n_w + i}),
        (z, n_z, lambda i: {"dp": i * n_w + w}),
    ):
        if count > 1:
            phases.append((len(phases), mine, count, where))

    barrier = pltpu.get_barrier_semaphore()
    greeted = 0
    for _, mine, count, where in phases:
        for off in range(1, count):
            pl.semaphore_signal(
                barrier, inc=1, device_id=where(lax.rem(mine + off, count)), device_id_type=MESH
            )
            greeted += 1

    def quantize_head(h):
        for t, ref in enumerate((k_ref, v_ref)):
            x = ref[:, h * HD : (h + 1) * HD].astype(jnp.float32)
            value, by_x, by_c = quantize(x, clip_ref[t * kvh + h : t * kvh + h + 1, :])
            kv[h, t, 0:HD, :] = value.astype(jnp.bfloat16)
            dx[h, t] = by_x
            dc[h, t] = by_c

    def fwd(h, d):
        return pltpu.make_async_remote_copy(
            src_ref=kv.at[h, :, pl.ds(d * HD, HD), :],
            dst_ref=kv.at[h, :, pl.ds((d + 1) * HD, HD), :],
            send_sem=fs.at[h, d],
            recv_sem=fr.at[h, d],
            device_id={"seq": nxt},
            device_id_type=MESH,
        )

    def bwd(h, t):
        return pltpu.make_async_remote_copy(
            src_ref=sbuf.at[h, t - 1],
            dst_ref=rbuf.at[h, t - 1],
            send_sem=bs.at[h, t - 1],
            recv_sem=br.at[h, t - 1],
            device_id={"seq": prv},
            device_id_type=MESH,
        )

    def relay(h, d):
        fwd(h, d - 1).wait_recv()
        fwd(h, d).start()

    def give_back(h, t):
        total = part[h, :, :, t * HD : (t + 1) * HD]
        if t < BACK:
            bwd(h, t + 1).wait_recv()
            total = total + rbuf[h, t].astype(jnp.float32)
        sbuf[h, t - 1] = total.astype(jnp.bfloat16)
        bwd(h, t).start()

    def finish(h):
        bwd(h, 1).wait_recv()
        here = pl.ds(pl.multiple_of(h * HD, HD), HD)
        for t, ref in enumerate((gk_ref, gv_ref)):
            total = part[h, t, :, 0:HD] + rbuf[h, 0, t].astype(jnp.float32)
            total = total.T
            if t == 0:
                total = total * SCALE
            ref[:, here] = (total * dx[h, t]).astype(ref.dtype)
            ar_src[0, pl.ds(t * kvh + h, 1), :] = jnp.sum(total * dc[h, t], axis=0, keepdims=True)

    quantize_head(0)
    pl.semaphore_wait(barrier, greeted)
    fwd(0, 0).start()
    quantize_head(1)
    fwd(1, 0).start()
    quantize_head(2)
    relay(0, 1)
    fwd(2, 0).start()
    quantize_head(3)

    row = lax.broadcasted_iota(jnp.int32, (HD, WIN), 0) + me * HD
    col = lax.broadcasted_iota(jnp.int32, (HD, WIN), 1)
    key = me * HD + lax.rem(col, HD) - (col // HD) * HD
    end = jnp.int32(0)
    first = jnp.zeros((HD, WIN), jnp.int32)
    for i in range(doc_ref.shape[1]):
        end = end + doc_ref[0, i]
        first = jnp.where(row >= end, end, first)
    bias[...] = jnp.where((key >= first) & (key <= row), 0.0, -1e30)

    relay(0, 2)
    relay(1, 1)
    relay(0, 3)

    steps = per_kv // (GROUP * HD)

    def one_head(h, _):
        def after(step):
            if step == 0:

                @pl.when(h + 3 < kvh)
                def _():
                    fwd(h + 3, 0).start()

                @pl.when(h + 1 < kvh)
                def _():
                    relay(h + 1, 2)

                @pl.when(h >= 1)
                def _():
                    give_back(h - 1, 3)

            if step == steps // 4:

                @pl.when(h + 2 < kvh)
                def _():
                    relay(h + 2, 1)

                @pl.when(h >= 1)
                def _():
                    give_back(h - 1, 2)

            if step == steps // 2:

                @pl.when(h + 1 < kvh)
                def _():
                    relay(h + 1, 3)

                @pl.when(h >= 1)
                def _():
                    give_back(h - 1, 1)

            if step == steps - 1:
                give_back(h, 4)

                @pl.when(h >= 2)
                def _():
                    finish(h - 2)

        for copy in loads(h):
            copy.wait()
        fwd(h, 3).wait_recv()
        for step in range(steps):
            lanes = [
                slice((step * GROUP + i) * HD, (step * GROUP + i + 1) * HD) for i in range(GROUP)
            ]
            q = jnp.concatenate([q_buf[h, :, at] for at in lanes], axis=0)
            g = jnp.concatenate([g_buf[h, :, at] for at in lanes], axis=0)
            out, dq, dk_t, dv_t = attend_step(q, g, kv[h, 0], kv[h, 1], bias[...])
            for i, at in enumerate(lanes):
                o_buf[h, :, at] = out[i * HD : (i + 1) * HD].astype(jnp.bfloat16)
                dq_buf[h, :, at] = dq[i * HD : (i + 1) * HD].astype(jnp.bfloat16)
            if step == 0:
                part[h, 0] = dk_t
                part[h, 1] = dv_t
            else:
                part[h, 0] += dk_t
                part[h, 1] += dv_t
            if step == steps - 1:
                for copy in stores(h):
                    copy.start()
            after(step)
        return 0

    lax.fori_loop(0, kvh, one_head, 0)

    last = kvh - 1
    give_back(last, 3)
    finish(last - 1)
    give_back(last, 2)
    give_back(last, 1)
    finish(last)

    def exchange(phase, mine, count, where, off, slot):
        return pltpu.make_async_remote_copy(
            src_ref=ar_src.at[phase],
            dst_ref=ar_buf.at[phase, slot],
            send_sem=ars.at[phase, off],
            recv_sem=arr.at[phase, off],
            device_id=where(lax.rem(mine + off, count)),
            device_id_type=MESH,
        )

    for phase, mine, count, where in phases:
        for off in range(1, count):
            exchange(phase, mine, count, where, off, mine).start()
        ar_buf[phase, mine] = ar_src[phase]
        for off in range(1, count):
            source = lax.rem(mine + count - off, count)
            exchange(phase, mine, count, where, off, source).wait_recv()
        total = ar_buf[phase, 0]
        for i in range(1, count):
            total = total + ar_buf[phase, i]
        ar_src[phase + 1] = total
    gs_ref[...] = ar_src[len(phases)]

    for phase, mine, count, where in phases:
        for off in range(1, count):
            exchange(phase, mine, count, where, off, mine).wait_send()
    for h in range(kvh):
        for d in range(BACK):
            fwd(h, d).wait_send()
            bwd(h, d + 1).wait_send()
        for copy in stores(h):
            copy.wait()


def on_device(queries, keys, values, grad_out, quant_scale, doc_lengths):
    rows, width = queries.shape
    kvh = quant_scale.shape[1]
    per_kv = width // kvh
    bf16, f32 = jnp.bfloat16, jnp.float32
    dma = pltpu.SemaphoreType.DMA
    vmem = pl.BlockSpec(memory_space=pltpu.VMEM)
    hbm = pl.BlockSpec(memory_space=pl.ANY)
    out, dq, gk, gv, gs = pl.pallas_call(
        functools.partial(kernel, kvh),
        out_shape=(
            jax.ShapeDtypeStruct(queries.shape, bf16),
            jax.ShapeDtypeStruct(queries.shape, bf16),
            jax.ShapeDtypeStruct(keys.shape, bf16),
            jax.ShapeDtypeStruct(values.shape, bf16),
            jax.ShapeDtypeStruct((2 * kvh, HD), f32),
        ),
        in_specs=[hbm, hbm, vmem, vmem, vmem, pl.BlockSpec(memory_space=pltpu.SMEM)],
        out_specs=(hbm, hbm, vmem, vmem, vmem),
        scratch_shapes=[
            pltpu.VMEM((kvh, rows, per_kv), bf16),
            pltpu.VMEM((kvh, rows, per_kv), bf16),
            pltpu.VMEM((kvh, rows, per_kv), bf16),
            pltpu.VMEM((kvh, rows, per_kv), bf16),
            pltpu.VMEM((kvh, 2, WIN, HD), bf16),
            pltpu.VMEM((kvh, 2, HD, WIN), f32),
            pltpu.VMEM((kvh, BACK, 2, HD, HD), bf16),
            pltpu.VMEM((kvh, BACK, 2, HD, HD), bf16),
            pltpu.VMEM((HD, WIN), f32),
            pltpu.VMEM((kvh, 2, rows, HD), f32),
            pltpu.VMEM((kvh, 2, rows, HD), f32),
            pltpu.VMEM((4, 2 * kvh, HD), f32),
            pltpu.VMEM((3, 8, 2 * kvh, HD), f32),
            dma((kvh, 2)),
            dma((kvh, 2)),
            dma((kvh, BACK)),
            dma((kvh, BACK)),
            dma((kvh, BACK)),
            dma((kvh, BACK)),
            dma((3, 8)),
            dma((3, 8)),
        ],
        compiler_params=pltpu.CompilerParams(
            collective_id=0, has_side_effects=True, vmem_limit_bytes=48 * 2**20
        ),
    )(queries, grad_out, keys, values, quant_scale.reshape(2 * kvh, HD), doc_lengths)
    return (out, dq, gk, gv, gs.reshape(quant_scale.shape))


def solution(mesh):
    rows = P(("dp", "seq"), None)
    return jax.shard_map(
        on_device,
        mesh=mesh,
        in_specs=(rows, rows, rows, rows, P(), P("dp", None)),
        out_specs=(rows, rows, rows, rows, P()),
        check_vma=False,
    )
```
